32 devices in a mesh: groups: 2 (over y), dp: 2 (over core), tensor: 8 (over z, x).
Axes of the slice: x: 2, y: 2, z: 4, core: 2. Of those that a mesh axis runs over, the one named last changes fastest.
Arguments:
- activations: bfloat16 [2048, 14336], P(('groups', 'dp'), 'tensor'), parts along dimension 0, may hold values from -6 to 6
- base_weight: bfloat16 [14336, 8192], P('tensor'), may hold values from -0.046875 to 0.046875
- adapter_down: bfloat16 [32, 16, 14336], P(('groups', 'tensor')), parts along dimension 0, may hold values from -0.046875 to 0.046875
- adapter_up: bfloat16 [32, 16, 8192], P(('groups', 'tensor')), parts along dimension 0, may hold values from -1.5 to 1.5
- block_adapter: int32 [4, 64], P(('groups', 'dp')), parts along dimension 0, may hold values from 0 to 15, as said below
- block_live: int32 [4, 64], P(('groups', 'dp')), parts along dimension 0, may hold values from 1 to 8, 320 in all within a row
- cotangent: bfloat16 [2048, 8192], P(('groups', 'dp'), 'tensor'), parts along dimension 0, may hold values from -6 to 6
Outputs:
- layer_out: bfloat16 [2048, 8192], P(('groups', 'dp'), 'tensor'), parts along dimension 0
- grad_input: bfloat16 [2048, 14336], P(('groups', 'dp'), 'tensor'), parts along dimension 0
- grad_down: bfloat16 [32, 16, 14336], P(('groups', 'tensor')), parts along dimension 0
- grad_up: bfloat16 [32, 16, 8192], P(('groups', 'tensor')), parts along dimension 0
The draws below stay inside these ranges and needn't reach their ends.
There are 2 independent parts, one for each index of `groups`. The reference program is written for one: setup_inputs(seed, part) draws one part's arguments, and reference() takes and returns one part's arrays. A program takes and returns all parts, laid end to end along the dimension named above; an argument that names none is the same for every part. Nothing has to cross between parts.
Inputs may be any that keep to these rules, and one draw needn't show every extreme that they name: `block_adapter`: index t of tensor owns the adapters t * 2 to (t + 1) * 2 - 1; in each row group the adapters of every owner name exactly 8 blocks. `block_live`: in each row group the entries add up to 320.
All inputs are finite; a program needn't handle non-finite values.
Results may differ from the reference program's by a relative error of at most 0.0051.
Values may be sent and summed in bfloat16 or wider, within the bound.
A program may use at most 256 MiB of HBM per device.

```python
import math
import jax
import jax.numpy as jnp
import numpy as np

MODEL_WIDTH = 8192
FF = 14336
RANK = 16
BLOCKS = 64
BLK = 8
ADP_DEV = 2
ADAPTERS = 16
TOKENS = 1024
LIVE = 320
N_DP = 2


def shuffled(group_key):
    return jax.random.permutation(group_key, BLOCKS)


def draw_block_adapter(key, part):
    key = jax.random.fold_in(key, 7)
    owner_key, first_key, second_key = jax.random.split(key, 3)
    owners = ADAPTERS // ADP_DEV
    group_keys = jax.random.split(owner_key, N_DP)
    orders = jax.vmap(shuffled)(group_keys).astype(jnp.int32)
    owner_of = orders % owners
    first_pick = jax.random.randint(first_key, (N_DP, BLOCKS), 0, ADP_DEV)
    second_pick = jax.random.randint(second_key, (N_DP, BLOCKS), 0, ADP_DEV)
    return (owner_of * ADP_DEV + jnp.minimum(first_pick, second_pick)).astype(jnp.int32)


def steps_of(own_key, shape, cuts, smallest, top_value):
    level = 1.0
    for position, blocks in cuts:
        draws = jax.random.uniform(jax.random.fold_in(jax.random.fold_in(own_key, 6), position), (blocks,), jnp.float32, smallest / len(cuts), top_value / len(cuts))
        level = level * jnp.repeat(jnp.exp(draws), shape[position] // blocks).reshape((-1,) + (1,) * (len(shape) - 1 - position))
    return level


def profile(amount, total, limit, lean):
    loads = [(1 << 20) // math.isqrt(rank ** lean) + 1 for rank in range(2, amount + 1)]
    rest, given = total - limit - (amount - 1), [1] * (amount - 1)
    while rest > 0:
        movable = [i for i in range(amount - 1) if given[i] < limit]
        whole, budget = sum([loads[i] for i in movable]), rest
        for i in movable:
            extra = min(limit - given[i], max(1, budget * loads[i] // whole), rest)
            given[i] = given[i] + extra
            rest = rest - extra
    return np.array([limit] + given)


def ragged_sizes(key, amount, total, reach, lean):
    if amount == 2:
        one = jax.random.randint(key, (), max(1, total - reach), min(reach, total - 1) + 1)
        return jnp.stack([one, total - one])
    sizes = jnp.asarray(profile(amount, total, reach, lean), jnp.int32)
    pairs = (amount - 1) // 2
    source_of, receiver = sizes[1:1 + 2 * pairs:2], sizes[2:2 + 2 * pairs:2]
    room = jnp.minimum(source_of - 1, reach - receiver)
    passed = jax.random.randint(jax.random.fold_in(key, 1), (pairs,), 0, 1 << 20) % (room + 1)
    sizes = sizes.at[1:1 + 2 * pairs:2].set(source_of - passed).at[2:2 + 2 * pairs:2].set(receiver + passed)
    return sizes[jax.random.permutation(jax.random.fold_in(key, 2), amount)]


def normal_values(key, extent, spread, bound, cuts=(), kind=jnp.bfloat16):
    values = spread * jax.random.normal(key, extent, jnp.float32)
    if cuts:
        values = values * steps_of(key, extent, cuts, -0.22, 0.18)
    return jnp.clip(values, -bound, bound).astype(kind)


def setup_inputs(seed: int = 0, part: int = 0) -> dict:
    splits = jax.random.split(jax.random.key(seed), 8)
    own_keys = jax.random.split(jax.random.fold_in(splits[7], part), 8)
    return {
        "activations": normal_values(own_keys[0], (TOKENS, FF), 1.0, 6.0, ((0, 2), (1, 8))),
        "base_weight": normal_values(splits[1], (FF, MODEL_WIDTH), FF ** -0.5, 0.046875, ((0, 8),)),
        "adapter_down": normal_values(own_keys[2], (ADAPTERS, RANK, FF), FF ** -0.5, 0.046875, ((0, 8),)),
        "adapter_up": normal_values(own_keys[3], (ADAPTERS, RANK, MODEL_WIDTH), RANK ** -0.5, 1.5, ((0, 8),)),
        "block_adapter": draw_block_adapter(jax.random.fold_in(jax.random.fold_in(splits[7], part), 71), part),
        "block_live": jax.vmap(lambda own: ragged_sizes(own, BLOCKS, LIVE, BLK, 1))(jax.random.split(own_keys[5], N_DP)).reshape((N_DP, BLOCKS)).astype(jnp.int32),
        "cotangent": normal_values(own_keys[6], (TOKENS, MODEL_WIDTH), 1.0, 6.0, ((0, 2), (1, 8))),
    }


lowrank_scale = 0.5


def reference(activations, base_weight, adapter_down, adapter_up, block_adapter, block_live, cotangent):
    block_ids = block_adapter.reshape(-1).astype(jnp.int32)
    block_count = block_ids.shape[0]
    positions = jnp.arange(BLK, dtype=jnp.int32)
    live = (positions[None, :] < block_live.reshape(-1)[:, None]).astype(jnp.float32)
    live_rows = live.reshape(-1, 1)
    act_blocks = activations.astype(jnp.float32).reshape(block_count, BLK, FF)
    down_blocks = adapter_down[block_ids].astype(jnp.float32)
    up_block_list = adapter_up[block_ids].astype(jnp.float32)
    lowrank_product = jnp.einsum("brf,bkf->brk", act_blocks, down_blocks).astype(jnp.bfloat16)
    base = jnp.dot(activations, base_weight, preferred_element_type=jnp.float32)
    adapter_output = jnp.einsum("nex,nxt->net", lowrank_product.astype(jnp.float32), up_block_list).reshape(-1, MODEL_WIDTH)
    layer_out = (live_rows * (base + lowrank_scale * adapter_output)).astype(jnp.bfloat16)
    masked = (cotangent.astype(jnp.float32) * live_rows).astype(jnp.bfloat16)
    masked_block_list = masked.astype(jnp.float32).reshape(block_count, BLK, MODEL_WIDTH)
    backward_result = (lowrank_scale * jnp.einsum("gys,gms->gym", masked_block_list, up_block_list)).astype(jnp.bfloat16)
    back_f = backward_result.astype(jnp.float32)
    through_base = jnp.dot(masked, base_weight.T, preferred_element_type=jnp.float32)
    through_adapter = jnp.einsum("brk,bkf->brf", back_f, down_blocks).reshape(-1, FF)
    grad_input = (through_base + through_adapter).astype(jnp.bfloat16)
    down_terms = jnp.einsum("brk,brf->bkf", back_f, act_blocks)
    up_projection_terms = lowrank_scale * jnp.einsum("svu,svj->suj", lowrank_product.astype(jnp.float32), masked_block_list)
    grad_down = jax.ops.segment_sum(down_terms, block_ids, num_segments=ADAPTERS).astype(jnp.bfloat16)
    grad_up = jax.ops.segment_sum(up_projection_terms, block_ids, num_segments=ADAPTERS).astype(jnp.bfloat16)
    return layer_out, grad_input, grad_down, grad_up
```

```python
import functools

import jax
import jax.numpy as jnp
from jax import lax
from jax.experimental import pallas as pl
from jax.experimental.pallas import tpu as pltpu
from jax.sharding import PartitionSpec as P

lowrank_scale = 0.5
live_total = 320

F32 = jnp.float32
BF16 = jnp.bfloat16


def dot(a, b, ca, cb):
    return lax.dot_general(a, b, (((ca,), (cb,)), ((), ())), preferred_element_type=F32)


def forward_kernel(x_ref, w_ref, out_ref):
    out_ref[0] = dot(x_ref[...], w_ref[...], 1, 0).astype(BF16)


def backward_kernel(g_ref, w_ref, rank_ref, down_ref, place_ref, out_ref, acc_ref):
    step = pl.program_id(0)

    @pl.when(step == 0)
    def _():
        acc_ref[...] = dot(rank_ref[...], down_ref[...], 1, 0)

    acc_ref[...] += dot(g_ref[0], w_ref[...], 1, 1)

    @pl.when(step == pl.num_programs(0) - 1)
    def _():
        rows = acc_ref[...].astype(BF16)
        out_ref[...] = dot(place_ref[...], rows, 0, 0).astype(BF16)


def body(activations, base_weight, adapter_down, adapter_up, block_adapter, block_live, cotangent):
    tensor_count = lax.axis_size("tensor")
    row_count, ff_dev = activations.shape
    d_dev = cotangent.shape[1]
    own_count, rank, _ = adapter_down.shape
    own_rows = own_count * rank
    wide = own_rows * tensor_count
    ids = block_adapter.reshape(-1)
    block_count = ids.shape[0]
    block_rows = row_count // block_count
    counts = block_live.reshape(-1)

    block_iota = jnp.arange(block_count, dtype=jnp.int32)
    first = jnp.sum(
        jnp.where(block_iota[None, :] < block_iota[:, None], counts[None, :], 0), axis=1
    )
    row_iota = jnp.arange(block_rows, dtype=jnp.int32)
    target = jnp.where(
        row_iota[None, :] < counts[:, None], first[:, None] + row_iota[None, :], -1
    ).reshape(1, row_count)
    live_iota = jnp.arange(live_total, dtype=jnp.int32)[:, None]
    place = (live_iota == target).astype(BF16)
    in_block = (live_iota >= first[None, :]) & (live_iota < (first + counts)[None, :])
    row_adapter = jnp.sum(jnp.where(in_block, ids[None, :], 0), axis=1, keepdims=True)
    wide_iota = jnp.arange(wide, dtype=jnp.int32)
    picked = row_adapter == (wide_iota // rank)[None, :]
    fold = ((wide_iota % rank)[:, None] == jnp.arange(rank, dtype=jnp.int32)[None, :]).astype(F32)

    grads = dot(place, cotangent, 1, 0).astype(BF16)
    grads_all = lax.all_gather(grads, "tensor", axis=0, tiled=False)
    acts = dot(place, activations, 1, 0).astype(BF16)

    send = jnp.concatenate(
        [
            adapter_down.reshape(own_rows, tensor_count, ff_dev),
            adapter_up.reshape(own_rows, tensor_count, d_dev),
        ],
        axis=2,
    ).transpose(1, 0, 2)
    adapters = lax.all_to_all(send, "tensor", split_axis=0, concat_axis=0, tiled=True)
    adapters = adapters.reshape(wide, ff_dev + d_dev)
    down_all, up_all = adapters[:, :ff_dev], adapters[:, ff_dev:]

    low_wide = jnp.where(picked, dot(acts, down_all, 1, 1), 0.0)
    back_wide = jnp.where(picked, dot(grads, up_all, 1, 1), 0.0)
    both = jnp.concatenate([low_wide, back_wide], axis=0)
    both = lax.dot_general(
        both, fold, (((1,), (0,)), ((), ())), precision=lax.Precision.HIGHEST,
        preferred_element_type=F32,
    )
    both = lax.psum(both, "tensor")
    low = both[:live_total].astype(BF16)
    back = (lowrank_scale * both[live_total:]).astype(BF16)
    fold_bf = fold.astype(BF16)
    low_spread = jnp.where(picked, dot(low, fold_bf, 1, 1), 0.0).astype(BF16)
    back_spread = jnp.where(picked, dot(back, fold_bf, 1, 1), 0.0).astype(BF16)

    params = pltpu.CompilerParams(vmem_limit_bytes=48 * 1024 * 1024)
    partial = pl.pallas_call(
        forward_kernel,
        grid=(tensor_count,),
        in_specs=[
            pl.BlockSpec((live_total, ff_dev), lambda j: (0, 0)),
            pl.BlockSpec((ff_dev, d_dev), lambda j: (0, j)),
        ],
        out_specs=pl.BlockSpec((1, live_total, d_dev), lambda j: (j, 0, 0)),
        out_shape=jax.ShapeDtypeStruct((tensor_count, live_total, d_dev), BF16),
        compiler_params=params,
    )(acts, base_weight)
    parts = lax.all_to_all(partial, "tensor", split_axis=0, concat_axis=0, tiled=True)

    grad_input = pl.pallas_call(
        backward_kernel,
        grid=(tensor_count,),
        in_specs=[
            pl.BlockSpec((1, live_total, d_dev), lambda j: (j, 0, 0)),
            pl.BlockSpec((ff_dev, d_dev), lambda j: (0, j)),
            pl.BlockSpec((live_total, wide), lambda j: (0, 0)),
            pl.BlockSpec((wide, ff_dev), lambda j: (0, 0)),
            pl.BlockSpec((live_total, row_count), lambda j: (0, 0)),
        ],
        out_specs=pl.BlockSpec((row_count, ff_dev), lambda j: (0, 0)),
        out_shape=jax.ShapeDtypeStruct((row_count, ff_dev), BF16),
        scratch_shapes=[pltpu.VMEM((live_total, ff_dev), F32)],
        compiler_params=params,
    )(grads_all, base_weight, back_spread, down_all, place)

    own_grads = jnp.concatenate(
        [dot(back_spread, acts, 0, 0), lowrank_scale * dot(low_spread, grads, 0, 0)], axis=1
    )
    own_grads = lax.psum(own_grads, "dp").astype(BF16)
    home = lax.all_to_all(
        own_grads.reshape(tensor_count, own_rows, ff_dev + d_dev),
        "tensor", split_axis=0, concat_axis=0, tiled=True,
    )
    down_own = home[:, :, :ff_dev].transpose(1, 0, 2).reshape(adapter_down.shape)
    up_own = home[:, :, ff_dev:].transpose(1, 0, 2).reshape(adapter_up.shape)

    base = jnp.sum(parts.astype(F32), axis=0)
    layer = (base + lowrank_scale * dot(low_spread, up_all, 1, 0)).astype(BF16)
    layer_out = dot(place, layer, 0, 0).astype(BF16)
    return layer_out, grad_input, down_own, up_own


def solution(mesh):
    in_specs = (
        P(("groups", "dp"), "tensor"),
        P("tensor", None),
        P(("groups", "tensor"), None, None),
        P(("groups", "tensor"), None, None),
        P(("groups", "dp"), None),
        P(("groups", "dp"), None),
        P(("groups", "dp"), "tensor"),
    )
    out_specs = (
        P(("groups", "dp"), "tensor"),
        P(("groups", "dp"), "tensor"),
        P(("groups", "tensor"), None, None),
        P(("groups", "tensor"), None, None),
    )
    return jax.shard_map(body, mesh=mesh, in_specs=in_specs, out_specs=out_specs, check_vma=False)
```

```python
import functools

import jax
import jax.numpy as jnp
from jax import lax
from jax.experimental import pallas as pl
from jax.experimental.pallas import tpu as pltpu
from jax.sharding import PartitionSpec as P

lowrank_scale = 0.5
live_total = 320

F32 = jnp.float32
BF16 = jnp.bfloat16


def dot(a, b, ca, cb):
    return lax.dot_general(a, b, (((ca,), (cb,)), ((), ())), preferred_element_type=F32)


def base_kernel(
    count, acts_ref, grads_ref, w_ref, base_ref, through_ref,
    gathered, pair_out, pair_in, line_out, line_in, kept, tiles, tile_sem,
    own_send, near_send, pass_send, gather_recv, pair_send, pair_recv, line_send, line_recv,
):
    d_dev = grads_ref.shape[1]
    lines = count // 2
    me = lax.axis_index("tensor")
    p = lax.rem(me, 2)
    q = lax.div(me, 2)
    near = q * 2 + (1 - p)

    def ahead(k):
        return lax.rem(q + 1 + k, lines)

    def behind(k):
        return lax.rem(q - 1 - k + lines, lines)

    def tile(chunk, step):
        slot = lax.rem(step, 2)
        columns = pl.ds(pl.multiple_of(chunk * d_dev, d_dev), d_dev)
        return pltpu.make_async_copy(w_ref.at[:, columns], tiles.at[slot], tile_sem.at[slot])

    def chunk_of(step):
        k = lax.rem(step, lines)
        back_side = jnp.where(step < 3 * lines, p, 1 - p)
        line = jnp.where(step < 2 * lines, ahead(k), lax.rem(q - k + lines, lines))
        side = jnp.where(step < lines, 1 - p, jnp.where(step < 2 * lines, p, back_side))
        return line * 2 + side

    def weights(step):
        @pl.when(step + 1 < 4 * lines)
        def _():
            tile(chunk_of(step + 1), step + 1).start()

        tile(chunk_of(step), step).wait()
        return tiles[lax.rem(step, 2)]

    def remote(src, dst, send, recv, target):
        return pltpu.make_async_remote_copy(
            src_ref=src, dst_ref=dst, send_sem=send, recv_sem=recv,
            device_id={"tensor": target}, device_id_type=pl.DeviceIdType.MESH,
        )

    def own_copy(k):
        target = ahead(k) * 2 + p
        return remote(grads_ref, gathered.at[me], own_send.at[k], gather_recv.at[me], target)

    def near_copy():
        return remote(grads_ref, gathered.at[me], near_send, gather_recv.at[me], near)

    def pass_copy(k):
        chunk = behind(k) * 2 + p
        return remote(
            gathered.at[chunk], gathered.at[chunk], pass_send.at[k], gather_recv.at[chunk], near
        )

    def arrival(chunk):
        return remote(grads_ref, gathered.at[chunk], near_send, gather_recv.at[chunk], near)

    def pair_copy(k):
        return remote(pair_out.at[k], pair_in.at[k], pair_send.at[k], pair_recv.at[k], near)

    def line_copy(k):
        target = ahead(k) * 2 + p
        return remote(line_out.at[k], line_in.at[k], line_send.at[k], line_recv.at[k], target)

    tile(chunk_of(0), 0).start()
    barrier = pltpu.get_barrier_semaphore()

    def greet(target):
        pl.semaphore_signal(
            barrier, inc=1, device_id={"tensor": target}, device_id_type=pl.DeviceIdType.MESH
        )

    greet(near)

    @pl.loop(0, lines - 1)
    def _(k):
        greet(ahead(k) * 2 + p)

    pl.semaphore_wait(barrier, lines)

    @pl.loop(0, lines - 1)
    def _(k):
        own_copy(k).start()

    @pl.loop(0, lines)
    def _(k):
        w = weights(k)
        pair_out[k] = dot(acts_ref[...], w, 1, 0).astype(BF16)
        pair_copy(k).start()

    near_copy().start()
    gathered[me] = grads_ref[...]

    @pl.loop(0, lines)
    def _(k):
        w = weights(lines + k)
        kept[...] = dot(acts_ref[...], w, 1, 0)
        pair_copy(k).wait_recv()

        @pl.when(k < lines - 1)
        def _():
            line_out[k] = (kept[...] + pair_in[k].astype(F32)).astype(BF16)
            line_copy(k).start()
            arrival(behind(k) * 2 + p).wait_recv()
            pass_copy(k).start()

    base_ref[...] = kept[...] + pair_in[lines - 1].astype(F32)
    through_ref[...] = jnp.zeros_like(through_ref)

    @pl.loop(0, 2 * lines)
    def _(k):
        chunk = chunk_of(2 * lines + k)

        @pl.when(k >= lines)
        def _():
            arrival(chunk).wait_recv()

        w = weights(2 * lines + k)
        through_ref[...] += dot(gathered[chunk], w, 1, 1)

    @pl.loop(0, lines - 1)
    def _(k):
        line_copy(k).wait_recv()
        base_ref[...] += line_in[k].astype(F32)
        line_copy(k).wait_send()
        own_copy(k).wait_send()
        pass_copy(k).wait_send()

    near_copy().wait_send()

    @pl.loop(0, lines)
    def _(k):
        pair_copy(k).wait_send()


def base_products(count, acts, grads, base_weight):
    rows, ff_dev = acts.shape
    d_dev = grads.shape[1]
    lines = count // 2
    vmem = pl.BlockSpec(memory_space=pltpu.VMEM)
    dma = pltpu.SemaphoreType.DMA
    return pl.pallas_call(
        functools.partial(base_kernel, count),
        in_specs=[vmem, vmem, pl.BlockSpec(memory_space=pl.ANY)],
        out_specs=[vmem, vmem],
        out_shape=[
            jax.ShapeDtypeStruct((rows, d_dev), F32),
            jax.ShapeDtypeStruct((rows, ff_dev), F32),
        ],
        scratch_shapes=[
            pltpu.VMEM((count, rows, d_dev), BF16),
            pltpu.VMEM((lines, rows, d_dev), BF16),
            pltpu.VMEM((lines, rows, d_dev), BF16),
            pltpu.VMEM((lines, rows, d_dev), BF16),
            pltpu.VMEM((lines, rows, d_dev), BF16),
            pltpu.VMEM((rows, d_dev), F32),
            pltpu.VMEM((2, ff_dev, d_dev), BF16),
            dma((2,)),
            dma((lines,)), dma, dma((lines,)), dma((count,)),
            dma((lines,)), dma((lines,)), dma((lines,)), dma((lines,)),
        ],
        compiler_params=pltpu.CompilerParams(
            collective_id=0, has_side_effects=True, vmem_limit_bytes=52 * 1024 * 1024
        ),
        cost_estimate=pl.CostEstimate(
            flops=4 * rows * ff_dev * d_dev * count,
            bytes_accessed=10 * ff_dev * d_dev * count,
            transcendentals=0,
        ),
    )(acts, grads, base_weight)


def body(activations, base_weight, adapter_down, adapter_up, block_adapter, block_live, cotangent):
    tensor_count = lax.axis_size("tensor")
    row_count, ff_dev = activations.shape
    d_dev = cotangent.shape[1]
    own_count, rank, _ = adapter_down.shape
    own_rows = own_count * rank
    wide = own_rows * tensor_count
    ids = block_adapter.reshape(-1)
    block_count = ids.shape[0]
    block_rows = row_count // block_count
    counts = block_live.reshape(-1)

    block_iota = jnp.arange(block_count, dtype=jnp.int32)
    first = jnp.sum(
        jnp.where(block_iota[None, :] < block_iota[:, None], counts[None, :], 0), axis=1
    )
    row_iota = jnp.arange(block_rows, dtype=jnp.int32)
    target = jnp.where(
        row_iota[None, :] < counts[:, None], first[:, None] + row_iota[None, :], -1
    ).reshape(1, row_count)
    live_iota = jnp.arange(live_total, dtype=jnp.int32)[:, None]
    place = (live_iota == target).astype(BF16)
    in_block = (live_iota >= first[None, :]) & (live_iota < (first + counts)[None, :])
    row_adapter = jnp.sum(jnp.where(in_block, ids[None, :], 0), axis=1, keepdims=True)
    wide_iota = jnp.arange(wide, dtype=jnp.int32)
    picked = row_adapter == (wide_iota // rank)[None, :]
    fold = ((wide_iota % rank)[:, None] == jnp.arange(rank, dtype=jnp.int32)[None, :]).astype(F32)

    grads = dot(place, cotangent, 1, 0).astype(BF16)
    acts = dot(place, activations, 1, 0).astype(BF16)

    send = jnp.concatenate(
        [
            adapter_down.reshape(own_rows, tensor_count, ff_dev),
            adapter_up.reshape(own_rows, tensor_count, d_dev),
        ],
        axis=2,
    ).transpose(1, 0, 2)
    adapters = lax.all_to_all(send, "tensor", split_axis=0, concat_axis=0, tiled=True)
    base, through = base_products(tensor_count, acts, grads, base_weight)
    adapters = adapters.reshape(wide, ff_dev + d_dev)
    down_all, up_all = adapters[:, :ff_dev], adapters[:, ff_dev:]

    low_wide = jnp.where(picked, dot(acts, down_all, 1, 1), 0.0)
    back_wide = jnp.where(picked, dot(grads, up_all, 1, 1), 0.0)
    both = jnp.concatenate([low_wide, back_wide], axis=0)
    both = lax.dot_general(
        both, fold, (((1,), (0,)), ((), ())), precision=lax.Precision.HIGHEST,
        preferred_element_type=F32,
    )
    both = lax.psum(both, "tensor")
    low = both[:live_total].astype(BF16)
    back = (lowrank_scale * both[live_total:]).astype(BF16)
    fold_bf = fold.astype(BF16)
    low_spread = jnp.where(picked, dot(low, fold_bf, 1, 1), 0.0).astype(BF16)
    back_spread = jnp.where(picked, dot(back, fold_bf, 1, 1), 0.0).astype(BF16)

    through = through + dot(back_spread, down_all, 1, 0)
    grad_input = dot(place, through.astype(BF16), 0, 0).astype(BF16)

    own_grads = jnp.concatenate(
        [dot(back_spread, acts, 0, 0), lowrank_scale * dot(low_spread, grads, 0, 0)], axis=1
    )
    own_grads = lax.psum(own_grads, "dp").astype(BF16)
    home = lax.all_to_all(
        own_grads.reshape(tensor_count, own_rows, ff_dev + d_dev),
        "tensor", split_axis=0, concat_axis=0, tiled=True,
    )
    down_own = home[:, :, :ff_dev].transpose(1, 0, 2).reshape(adapter_down.shape)
    up_own = home[:, :, ff_dev:].transpose(1, 0, 2).reshape(adapter_up.shape)

    layer = (base + lowrank_scale * dot(low_spread, up_all, 1, 0)).astype(BF16)
    layer_out = dot(place, layer, 0, 0).astype(BF16)
    return layer_out, grad_input, down_own, up_own


def solution(mesh):
    in_specs = (
        P(("groups", "dp"), "tensor"),
        P("tensor", None),
        P(("groups", "tensor"), None, None),
        P(("groups", "tensor"), None, None),
        P(("groups", "dp"), None),
        P(("groups", "dp"), None),
        P(("groups", "dp"), "tensor"),
    )
    out_specs = (
        P(("groups", "dp"), "tensor"),
        P(("groups", "dp"), "tensor"),
        P(("groups", "tensor"), None, None),
        P(("groups", "tensor"), None, None),
    )
    return jax.shard_map(body, mesh=mesh, in_specs=in_specs, out_specs=out_specs, check_vma=False)
```

```python
import functools

import jax
import jax.numpy as jnp
from jax import lax
from jax.experimental import pallas as pl
from jax.experimental.pallas import tpu as pltpu
from jax.sharding import PartitionSpec as P

lowrank_scale = 0.5
live_total = 320

F32 = jnp.float32
BF16 = jnp.bfloat16


def dot(a, b, ca, cb):
    return lax.dot_general(a, b, (((ca,), (cb,)), ((), ())), preferred_element_type=F32)


def base_kernel(
    count, acts_ref, grads_ref, w_ref, base_ref, through_ref,
    gathered, pair_out, pair_in, line_out, line_in, kept, tiles, tile_sem,
    up_send, down_send, near_send, pass_send, gather_recv, pair_send, pair_recv, line_send, line_recv,
):
    d_dev = grads_ref.shape[1]
    lines = count // 2
    me = lax.axis_index("tensor")
    p = lax.rem(me, 2)
    q = lax.div(me, 2)
    near = q * 2 + (1 - p)
    turn = jnp.where(q * 2 < lines, 1, -1)

    def ahead(k):
        return lax.rem(q + 1 + k, lines)

    def tile(chunk, step):
        slot = lax.rem(step, 2)
        columns = pl.ds(pl.multiple_of(chunk * d_dev, d_dev), d_dev)
        return pltpu.make_async_copy(w_ref.at[:, columns], tiles.at[slot], tile_sem.at[slot])

    def chunk_of(step):
        k = lax.rem(step, lines)
        back_side = jnp.where(step < 3 * lines, p, 1 - p)
        line = jnp.where(step < 2 * lines, ahead(k), lax.rem(q + turn * k + lines, lines))
        side = jnp.where(step < lines, 1 - p, jnp.where(step < 2 * lines, p, back_side))
        return line * 2 + side

    def weights(step):
        @pl.when(step + 1 < 4 * lines)
        def _():
            tile(chunk_of(step + 1), step + 1).start()

        tile(chunk_of(step), step).wait()
        return tiles[lax.rem(step, 2)]

    def remote(src, dst, send, recv, target):
        return pltpu.make_async_remote_copy(
            src_ref=src, dst_ref=dst, send_sem=send, recv_sem=recv,
            device_id={"tensor": target}, device_id_type=pl.DeviceIdType.MESH,
        )

    def near_copy():
        return remote(grads_ref, gathered.at[me], near_send, gather_recv.at[me], near)

    def pass_copy(line):
        chunk = line * 2 + p
        return remote(
            gathered.at[chunk], gathered.at[chunk], pass_send.at[line], gather_recv.at[chunk], near
        )

    def first_hop(sends, line):
        target = line * 2 + p
        return remote(grads_ref, gathered.at[me], sends.at[0], gather_recv.at[me], target)

    def hop(distance, source, sends, line):
        chunk = source * 2 + p
        return remote(
            gathered.at[chunk], gathered.at[chunk], sends.at[distance],
            gather_recv.at[chunk], line * 2 + p,
        )

    has_up = q + 1 < lines
    has_down = q > 0

    def arrival(chunk):
        return remote(grads_ref, gathered.at[chunk], near_send, gather_recv.at[chunk], near)

    def pair_copy(k):
        return remote(pair_out.at[k], pair_in.at[k], pair_send.at[k], pair_recv.at[k], near)

    def line_copy(k):
        target = ahead(k) * 2 + p
        return remote(line_out.at[k], line_in.at[k], line_send.at[k], line_recv.at[k], target)

    tile(chunk_of(0), 0).start()
    barrier = pltpu.get_barrier_semaphore()

    def greet(target):
        pl.semaphore_signal(
            barrier, inc=1, device_id={"tensor": target}, device_id_type=pl.DeviceIdType.MESH
        )

    greet(near)

    @pl.loop(0, lines - 1)
    def _(k):
        greet(ahead(k) * 2 + p)

    pl.semaphore_wait(barrier, lines)

    @pl.when(has_up)
    def _():
        first_hop(up_send, q + 1).start()

    @pl.when(has_down)
    def _():
        first_hop(down_send, q - 1).start()

    @pl.loop(0, lines)
    def _(k):
        w = weights(k)
        pair_out[k] = dot(acts_ref[...], w, 1, 0).astype(BF16)
        pair_copy(k).start()

    near_copy().start()
    gathered[me] = grads_ref[...]

    @pl.loop(0, lines)
    def _(k):
        w = weights(lines + k)
        kept[...] = dot(acts_ref[...], w, 1, 0)
        pair_copy(k).wait_recv()

        @pl.when(k < lines - 1)
        def _():
            line_out[k] = (kept[...] + pair_in[k].astype(F32)).astype(BF16)
            line_copy(k).start()
            below, above = q - 1 - k, q + 1 + k

            @pl.when(below >= 0)
            def _():
                arrival(below * 2 + p).wait_recv()

                @pl.when(has_up)
                def _():
                    hop(k + 1, below, up_send, q + 1).start()

                pass_copy(below).start()

            @pl.when(above < lines)
            def _():
                arrival(above * 2 + p).wait_recv()

                @pl.when(has_down)
                def _():
                    hop(k + 1, above, down_send, q - 1).start()

                pass_copy(above).start()

    base_ref[...] = kept[...] + pair_in[lines - 1].astype(F32)
    through_ref[...] = jnp.zeros_like(through_ref)

    @pl.loop(0, 2 * lines)
    def _(k):
        chunk = chunk_of(2 * lines + k)

        @pl.when(k >= lines)
        def _():
            arrival(chunk).wait_recv()

        w = weights(2 * lines + k)
        through_ref[...] += dot(gathered[chunk], w, 1, 1)

    @pl.loop(0, lines - 1)
    def _(k):
        line_copy(k).wait_recv()
        base_ref[...] += line_in[k].astype(F32)
        line_copy(k).wait_send()
        below, above = q - 1 - k, q + 1 + k

        @pl.when(below >= 0)
        def _():
            pass_copy(below).wait_send()

            @pl.when(has_up)
            def _():
                hop(k + 1, below, up_send, q + 1).wait_send()

        @pl.when(above < lines)
        def _():
            pass_copy(above).wait_send()

            @pl.when(has_down)
            def _():
                hop(k + 1, above, down_send, q - 1).wait_send()

    @pl.when(has_up)
    def _():
        first_hop(up_send, q + 1).wait_send()

    @pl.when(has_down)
    def _():
        first_hop(down_send, q - 1).wait_send()

    near_copy().wait_send()

    @pl.loop(0, lines)
    def _(k):
        pair_copy(k).wait_send()


def rank_kernel(count, part_ref, out_ref, pair_in, line_in, pair_send, pair_recv, line_send, line_recv):
    lines = count // 2
    me = lax.axis_index("tensor")
    p = lax.rem(me, 2)
    q = lax.div(me, 2)
    near = q * 2 + (1 - p)
    barrier = pltpu.get_barrier_semaphore()

    def ahead(k):
        return lax.rem(q + 1 + k, lines)

    def greet(target):
        pl.semaphore_signal(
            barrier, inc=1, device_id={"tensor": target}, device_id_type=pl.DeviceIdType.MESH
        )

    def line_copy(source, k, target):
        return pltpu.make_async_remote_copy(
            src_ref=line_in.at[source], dst_ref=line_in.at[source],
            send_sem=line_send.at[k], recv_sem=line_recv.at[source],
            device_id={"tensor": target * 2 + p}, device_id_type=pl.DeviceIdType.MESH,
        )

    greet(near)

    @pl.loop(0, lines - 1)
    def _(k):
        greet(ahead(k) * 2 + p)

    pl.semaphore_wait(barrier, lines)
    pair = pltpu.make_async_remote_copy(
        src_ref=part_ref, dst_ref=pair_in, send_sem=pair_send, recv_sem=pair_recv,
        device_id={"tensor": near}, device_id_type=pl.DeviceIdType.MESH,
    )
    pair.start()
    pair.wait()
    line_in[q] = part_ref[...] + pair_in[...]

    @pl.loop(0, lines - 1)
    def _(k):
        line_copy(q, k, ahead(k)).start()

    @pl.loop(0, lines - 1)
    def _(k):
        line_copy(ahead(k), k, ahead(k)).wait_recv()

    out_ref[...] = line_in[0]

    @pl.loop(1, lines)
    def _(k):
        out_ref[...] += line_in[k]

    @pl.loop(0, lines - 1)
    def _(k):
        line_copy(q, k, ahead(k)).wait_send()


def rank_sums(count, part):
    lines = count // 2
    vmem = pl.BlockSpec(memory_space=pltpu.VMEM)
    dma = pltpu.SemaphoreType.DMA
    return pl.pallas_call(
        functools.partial(rank_kernel, count),
        in_specs=[vmem],
        out_specs=vmem,
        out_shape=jax.ShapeDtypeStruct(part.shape, F32),
        scratch_shapes=[
            pltpu.VMEM(part.shape, F32),
            pltpu.VMEM((lines,) + part.shape, F32),
            dma, dma, dma((lines,)), dma((lines,)),
        ],
        compiler_params=pltpu.CompilerParams(
            collective_id=1, has_side_effects=True, vmem_limit_bytes=16 * 1024 * 1024
        ),
    )(part)


def base_products(count, acts, grads, base_weight):
    rows, ff_dev = acts.shape
    d_dev = grads.shape[1]
    lines = count // 2
    vmem = pl.BlockSpec(memory_space=pltpu.VMEM)
    dma = pltpu.SemaphoreType.DMA
    return pl.pallas_call(
        functools.partial(base_kernel, count),
        in_specs=[vmem, vmem, pl.BlockSpec(memory_space=pl.ANY)],
        out_specs=[vmem, vmem],
        out_shape=[
            jax.ShapeDtypeStruct((rows, d_dev), F32),
            jax.ShapeDtypeStruct((rows, ff_dev), F32),
        ],
        scratch_shapes=[
            pltpu.VMEM((count, rows, d_dev), BF16),
            pltpu.VMEM((lines, rows, d_dev), BF16),
            pltpu.VMEM((lines, rows, d_dev), BF16),
            pltpu.VMEM((lines, rows, d_dev), BF16),
            pltpu.VMEM((lines, rows, d_dev), BF16),
            pltpu.VMEM((rows, d_dev), F32),
            pltpu.VMEM((2, ff_dev, d_dev), BF16),
            dma((2,)),
            dma((lines,)), dma((lines,)), dma, dma((lines,)), dma((count,)),
            dma((lines,)), dma((lines,)), dma((lines,)), dma((lines,)),
        ],
        compiler_params=pltpu.CompilerParams(
            collective_id=0, has_side_effects=True, vmem_limit_bytes=52 * 1024 * 1024
        ),
        cost_estimate=pl.CostEstimate(
            flops=4 * rows * ff_dev * d_dev * count,
            bytes_accessed=10 * ff_dev * d_dev * count,
            transcendentals=0,
        ),
    )(acts, grads, base_weight)


def body(activations, base_weight, adapter_down, adapter_up, block_adapter, block_live, cotangent):
    tensor_count = lax.axis_size("tensor")
    row_count, ff_dev = activations.shape
    d_dev = cotangent.shape[1]
    own_count, rank, _ = adapter_down.shape
    own_rows = own_count * rank
    wide = own_rows * tensor_count
    ids = block_adapter.reshape(-1)
    block_count = ids.shape[0]
    block_rows = row_count // block_count
    counts = block_live.reshape(-1)

    block_iota = jnp.arange(block_count, dtype=jnp.int32)
    first = jnp.sum(
        jnp.where(block_iota[None, :] < block_iota[:, None], counts[None, :], 0), axis=1
    )
    row_iota = jnp.arange(block_rows, dtype=jnp.int32)
    target = jnp.where(
        row_iota[None, :] < counts[:, None], first[:, None] + row_iota[None, :], -1
    ).reshape(1, row_count)
    live_iota = jnp.arange(live_total, dtype=jnp.int32)[:, None]
    place = (live_iota == target).astype(BF16)
    in_block = (live_iota >= first[None, :]) & (live_iota < (first + counts)[None, :])
    row_adapter = jnp.sum(jnp.where(in_block, ids[None, :], 0), axis=1, keepdims=True)
    wide_iota = jnp.arange(wide, dtype=jnp.int32)
    picked = row_adapter == (wide_iota // rank)[None, :]
    fold = ((wide_iota % rank)[:, None] == jnp.arange(rank, dtype=jnp.int32)[None, :]).astype(F32)

    grads = dot(place, cotangent, 1, 0).astype(BF16)
    acts = dot(place, activations, 1, 0).astype(BF16)

    send = jnp.concatenate(
        [
            adapter_down.reshape(own_rows, tensor_count, ff_dev),
            adapter_up.reshape(own_rows, tensor_count, d_dev),
        ],
        axis=2,
    ).transpose(1, 0, 2)
    adapters = lax.all_to_all(send, "tensor", split_axis=0, concat_axis=0, tiled=True)
    base, through = base_products(tensor_count, acts, grads, base_weight)
    adapters = adapters.reshape(wide, ff_dev + d_dev)
    down_all, up_all = adapters[:, :ff_dev], adapters[:, ff_dev:]

    low_wide = jnp.where(picked, dot(acts, down_all, 1, 1), 0.0)
    back_wide = jnp.where(picked, dot(grads, up_all, 1, 1), 0.0)
    both = jnp.concatenate([low_wide, back_wide], axis=0)
    both = lax.dot_general(
        fold, both, (((0,), (1,)), ((), ())), precision=lax.Precision.HIGHEST,
        preferred_element_type=F32,
    )
    both = rank_sums(tensor_count, both)
    low = both[:, :live_total].astype(BF16)
    back = (lowrank_scale * both[:, live_total:]).astype(BF16)
    fold_bf = fold.astype(BF16)
    low_spread = jnp.where(picked, dot(low, fold_bf, 0, 1), 0.0).astype(BF16)
    back_spread = jnp.where(picked, dot(back, fold_bf, 0, 1), 0.0).astype(BF16)

    through = through + dot(back_spread, down_all, 1, 0)
    grad_input = dot(place, through.astype(BF16), 0, 0).astype(BF16)

    own_grads = jnp.concatenate(
        [dot(back_spread, acts, 0, 0), lowrank_scale * dot(low_spread, grads, 0, 0)], axis=1
    )
    own_grads = lax.psum(own_grads, "dp").astype(BF16)
    home = lax.all_to_all(
        own_grads.reshape(tensor_count, own_rows, ff_dev + d_dev),
        "tensor", split_axis=0, concat_axis=0, tiled=True,
    )
    down_own = home[:, :, :ff_dev].transpose(1, 0, 2).reshape(adapter_down.shape)
    up_own = home[:, :, ff_dev:].transpose(1, 0, 2).reshape(adapter_up.shape)

    layer = (base + lowrank_scale * dot(low_spread, up_all, 1, 0)).astype(BF16)
    layer_out = dot(place, layer, 0, 0).astype(BF16)
    return layer_out, grad_input, down_own, up_own


def solution(mesh):
    in_specs = (
        P(("groups", "dp"), "tensor"),
        P("tensor", None),
        P(("groups", "tensor"), None, None),
        P(("groups", "tensor"), None, None),
        P(("groups", "dp"), None),
        P(("groups", "dp"), None),
        P(("groups", "dp"), "tensor"),
    )
    out_specs = (
        P(("groups", "dp"), "tensor"),
        P(("groups", "dp"), "tensor"),
        P(("groups", "tensor"), None, None),
        P(("groups", "tensor"), None, None),
    )
    return jax.shard_map(body, mesh=mesh, in_specs=in_specs, out_specs=out_specs, check_vma=False)
```

```python
import functools

import jax
import jax.numpy as jnp
from jax import lax
from jax.experimental import pallas as pl
from jax.experimental.pallas import tpu as pltpu
from jax.sharding import PartitionSpec as P

lowrank_scale = 0.5
live_total = 320

F32 = jnp.float32
BF16 = jnp.bfloat16


def dot(a, b, ca, cb):
    return lax.dot_general(a, b, (((ca,), (cb,)), ((), ())), preferred_element_type=F32)


def base_kernel(
    count, acts_ref, grads_ref, w_ref, base_ref, through_ref,
    gathered, pair_out, pair_in, line_out, line_in, kept, tiles, tile_sem,
    up_send, down_send, near_send, pass_send, gather_recv, pair_send, pair_recv, line_send, line_recv,
):
    d_dev = grads_ref.shape[1]
    lines = count // 2
    me = lax.axis_index("tensor")
    p = lax.rem(me, 2)
    q = lax.div(me, 2)
    near = q * 2 + (1 - p)
    turn = jnp.where(q * 2 < lines, 1, -1)

    def ahead(k):
        return lax.rem(q + 1 + k, lines)

    def tile(chunk, step):
        slot = lax.rem(step, 2)
        columns = pl.ds(pl.multiple_of(chunk * d_dev, d_dev), d_dev)
        return pltpu.make_async_copy(w_ref.at[:, columns], tiles.at[slot], tile_sem.at[slot])

    def chunk_of(step):
        k = lax.rem(step, lines)
        back_side = jnp.where(step < 3 * lines, p, 1 - p)
        line = jnp.where(step < 2 * lines, ahead(k), lax.rem(q + turn * k + lines, lines))
        side = jnp.where(step < lines, 1 - p, jnp.where(step < 2 * lines, p, back_side))
        return line * 2 + side

    def weights(step):
        @pl.when(step + 1 < 4 * lines)
        def _():
            tile(chunk_of(step + 1), step + 1).start()

        tile(chunk_of(step), step).wait()
        return tiles[lax.rem(step, 2)]

    def remote(src, dst, send, recv, target):
        return pltpu.make_async_remote_copy(
            src_ref=src, dst_ref=dst, send_sem=send, recv_sem=recv,
            device_id={"tensor": target}, device_id_type=pl.DeviceIdType.MESH,
        )

    def near_copy():
        return remote(grads_ref, gathered.at[me], near_send, gather_recv.at[me], near)

    def pass_copy(line):
        chunk = line * 2 + p
        return remote(
            gathered.at[chunk], gathered.at[chunk], pass_send.at[line], gather_recv.at[chunk], near
        )

    def first_hop(sends, line):
        target = line * 2 + p
        return remote(grads_ref, gathered.at[me], sends.at[0], gather_recv.at[me], target)

    def hop(distance, source, sends, line):
        chunk = source * 2 + p
        return remote(
            gathered.at[chunk], gathered.at[chunk], sends.at[distance],
            gather_recv.at[chunk], line * 2 + p,
        )

    has_up = q + 1 < lines
    has_down = q > 0

    def arrival(chunk):
        return remote(grads_ref, gathered.at[chunk], near_send, gather_recv.at[chunk], near)

    def pair_copy(k):
        return remote(pair_out.at[k], pair_in.at[k], pair_send.at[k], pair_recv.at[k], near)

    def line_copy(k):
        target = ahead(k) * 2 + p
        return remote(line_out.at[k], line_in.at[k], line_send.at[k], line_recv.at[k], target)

    tile(chunk_of(0), 0).start()
    barrier = pltpu.get_barrier_semaphore()

    def greet(target):
        pl.semaphore_signal(
            barrier, inc=1, device_id={"tensor": target}, device_id_type=pl.DeviceIdType.MESH
        )

    greet(near)

    @pl.loop(0, lines - 1)
    def _(k):
        greet(ahead(k) * 2 + p)

    pl.semaphore_wait(barrier, lines)
    near_copy().start()

    @pl.when(has_up)
    def _():
        first_hop(up_send, q + 1).start()

    @pl.when(has_down)
    def _():
        first_hop(down_send, q - 1).start()

    gathered[me] = grads_ref[...]

    @pl.loop(0, lines)
    def _(k):
        w = weights(k)
        pair_out[k] = dot(acts_ref[...], w, 1, 0).astype(BF16)
        pair_copy(k).start()


    @pl.loop(0, lines)
    def _(k):
        w = weights(lines + k)
        kept[...] = dot(acts_ref[...], w, 1, 0)
        pair_copy(k).wait_recv()

        @pl.when(k < lines - 1)
        def _():
            line_out[k] = (kept[...] + pair_in[k].astype(F32)).astype(BF16)
            line_copy(k).start()
            below, above = q - 1 - k, q + 1 + k

            @pl.when(below >= 0)
            def _():
                arrival(below * 2 + p).wait_recv()

                @pl.when(has_up)
                def _():
                    hop(k + 1, below, up_send, q + 1).start()

                pass_copy(below).start()

            @pl.when(above < lines)
            def _():
                arrival(above * 2 + p).wait_recv()

                @pl.when(has_down)
                def _():
                    hop(k + 1, above, down_send, q - 1).start()

                pass_copy(above).start()

    base_ref[...] = kept[...] + pair_in[lines - 1].astype(F32)
    through_ref[...] = jnp.zeros_like(through_ref)

    @pl.loop(0, 2 * lines)
    def _(k):
        chunk = chunk_of(2 * lines + k)

        @pl.when(k >= lines)
        def _():
            arrival(chunk).wait_recv()

        w = weights(2 * lines + k)
        through_ref[...] += dot(gathered[chunk], w, 1, 1)

    @pl.loop(0, lines - 1)
    def _(k):
        line_copy(k).wait_recv()
        base_ref[...] += line_in[k].astype(F32)
        line_copy(k).wait_send()
        below, above = q - 1 - k, q + 1 + k

        @pl.when(below >= 0)
        def _():
            pass_copy(below).wait_send()

            @pl.when(has_up)
            def _():
                hop(k + 1, below, up_send, q + 1).wait_send()

        @pl.when(above < lines)
        def _():
            pass_copy(above).wait_send()

            @pl.when(has_down)
            def _():
                hop(k + 1, above, down_send, q - 1).wait_send()

    @pl.when(has_up)
    def _():
        first_hop(up_send, q + 1).wait_send()

    @pl.when(has_down)
    def _():
        first_hop(down_send, q - 1).wait_send()

    near_copy().wait_send()

    @pl.loop(0, lines)
    def _(k):
        pair_copy(k).wait_send()


def rank_kernel(count, part_ref, out_ref, pair_in, line_in, pair_send, pair_recv, line_send, line_recv):
    lines = count // 2
    me = lax.axis_index("tensor")
    p = lax.rem(me, 2)
    q = lax.div(me, 2)
    near = q * 2 + (1 - p)
    barrier = pltpu.get_barrier_semaphore()

    def ahead(k):
        return lax.rem(q + 1 + k, lines)

    def greet(target):
        pl.semaphore_signal(
            barrier, inc=1, device_id={"tensor": target}, device_id_type=pl.DeviceIdType.MESH
        )

    def line_copy(source, k, target):
        return pltpu.make_async_remote_copy(
            src_ref=line_in.at[source], dst_ref=line_in.at[source],
            send_sem=line_send.at[k], recv_sem=line_recv.at[source],
            device_id={"tensor": target * 2 + p}, device_id_type=pl.DeviceIdType.MESH,
        )

    greet(near)

    @pl.loop(0, lines - 1)
    def _(k):
        greet(ahead(k) * 2 + p)

    pl.semaphore_wait(barrier, lines)
    pair = pltpu.make_async_remote_copy(
        src_ref=part_ref, dst_ref=pair_in, send_sem=pair_send, recv_sem=pair_recv,
        device_id={"tensor": near}, device_id_type=pl.DeviceIdType.MESH,
    )
    pair.start()
    pair.wait()
    line_in[q] = part_ref[...] + pair_in[...]

    @pl.loop(0, lines - 1)
    def _(k):
        line_copy(q, k, ahead(k)).start()

    @pl.loop(0, lines - 1)
    def _(k):
        line_copy(ahead(k), k, ahead(k)).wait_recv()

    out_ref[...] = line_in[0]

    @pl.loop(1, lines)
    def _(k):
        out_ref[...] += line_in[k]

    @pl.loop(0, lines - 1)
    def _(k):
        line_copy(q, k, ahead(k)).wait_send()


def rank_sums(count, part):
    lines = count // 2
    vmem = pl.BlockSpec(memory_space=pltpu.VMEM)
    dma = pltpu.SemaphoreType.DMA
    return pl.pallas_call(
        functools.partial(rank_kernel, count),
        in_specs=[vmem],
        out_specs=vmem,
        out_shape=jax.ShapeDtypeStruct(part.shape, F32),
        scratch_shapes=[
            pltpu.VMEM(part.shape, F32),
            pltpu.VMEM((lines,) + part.shape, F32),
            dma, dma, dma((lines,)), dma((lines,)),
        ],
        compiler_params=pltpu.CompilerParams(
            collective_id=1, has_side_effects=True, vmem_limit_bytes=16 * 1024 * 1024
        ),
    )(part)


def base_products(count, acts, grads, base_weight):
    rows, ff_dev = acts.shape
    d_dev = grads.shape[1]
    lines = count // 2
    vmem = pl.BlockSpec(memory_space=pltpu.VMEM)
    dma = pltpu.SemaphoreType.DMA
    return pl.pallas_call(
        functools.partial(base_kernel, count),
        in_specs=[vmem, vmem, pl.BlockSpec(memory_space=pl.ANY)],
        out_specs=[vmem, vmem],
        out_shape=[
            jax.ShapeDtypeStruct((rows, d_dev), F32),
            jax.ShapeDtypeStruct((rows, ff_dev), F32),
        ],
        scratch_shapes=[
            pltpu.VMEM((count, rows, d_dev), BF16),
            pltpu.VMEM((lines, rows, d_dev), BF16),
            pltpu.VMEM((lines, rows, d_dev), BF16),
            pltpu.VMEM((lines, rows, d_dev), BF16),
            pltpu.VMEM((lines, rows, d_dev), BF16),
            pltpu.VMEM((rows, d_dev), F32),
            pltpu.VMEM((2, ff_dev, d_dev), BF16),
            dma((2,)),
            dma((lines,)), dma((lines,)), dma, dma((lines,)), dma((count,)),
            dma((lines,)), dma((lines,)), dma((lines,)), dma((lines,)),
        ],
        compiler_params=pltpu.CompilerParams(
            collective_id=0, has_side_effects=True, vmem_limit_bytes=52 * 1024 * 1024
        ),
        cost_estimate=pl.CostEstimate(
            flops=4 * rows * ff_dev * d_dev * count,
            bytes_accessed=10 * ff_dev * d_dev * count,
            transcendentals=0,
        ),
    )(acts, grads, base_weight)


def body(activations, base_weight, adapter_down, adapter_up, block_adapter, block_live, cotangent):
    tensor_count = lax.axis_size("tensor")
    row_count, ff_dev = activations.shape
    d_dev = cotangent.shape[1]
    own_count, rank, _ = adapter_down.shape
    own_rows = own_count * rank
    wide = own_rows * tensor_count
    ids = block_adapter.reshape(-1)
    block_count = ids.shape[0]
    block_rows = row_count // block_count
    counts = block_live.reshape(-1)

    block_iota = jnp.arange(block_count, dtype=jnp.int32)
    first = jnp.sum(
        jnp.where(block_iota[None, :] < block_iota[:, None], counts[None, :], 0), axis=1
    )
    row_iota = jnp.arange(block_rows, dtype=jnp.int32)
    target = jnp.where(
        row_iota[None, :] < counts[:, None], first[:, None] + row_iota[None, :], -1
    ).reshape(1, row_count)
    live_iota = jnp.arange(live_total, dtype=jnp.int32)[:, None]
    place = (live_iota == target).astype(BF16)
    in_block = (live_iota >= first[None, :]) & (live_iota < (first + counts)[None, :])
    row_adapter = jnp.sum(jnp.where(in_block, ids[None, :], 0), axis=1, keepdims=True)
    wide_iota = jnp.arange(wide, dtype=jnp.int32)
    picked = row_adapter == (wide_iota // rank)[None, :]
    fold = ((wide_iota % rank)[:, None] == jnp.arange(rank, dtype=jnp.int32)[None, :]).astype(F32)

    grads = dot(place, cotangent, 1, 0).astype(BF16)
    acts = dot(place, activations, 1, 0).astype(BF16)

    send = jnp.concatenate(
        [
            adapter_down.reshape(own_rows, tensor_count, ff_dev),
            adapter_up.reshape(own_rows, tensor_count, d_dev),
        ],
        axis=2,
    ).transpose(1, 0, 2)
    adapters = lax.all_to_all(send, "tensor", split_axis=0, concat_axis=0, tiled=True)
    base, through = base_products(tensor_count, acts, grads, base_weight)
    adapters = adapters.reshape(wide, ff_dev + d_dev)
    down_all, up_all = adapters[:, :ff_dev], adapters[:, ff_dev:]

    low_wide = jnp.where(picked, dot(acts, down_all, 1, 1), 0.0)
    back_wide = jnp.where(picked, dot(grads, up_all, 1, 1), 0.0)
    both = jnp.concatenate([low_wide, back_wide], axis=0)
    both = lax.dot_general(
        fold, both, (((0,), (1,)), ((), ())), precision=lax.Precision.HIGHEST,
        preferred_element_type=F32,
    )
    both = rank_sums(tensor_count, both)
    low = both[:, :live_total].astype(BF16)
    back = (lowrank_scale * both[:, live_total:]).astype(BF16)
    fold_bf = fold.astype(BF16)
    low_spread = jnp.where(picked, dot(low, fold_bf, 0, 1), 0.0).astype(BF16)
    back_spread = jnp.where(picked, dot(back, fold_bf, 0, 1), 0.0).astype(BF16)

    through = through + dot(back_spread, down_all, 1, 0)
    grad_input = dot(place, through.astype(BF16), 0, 0).astype(BF16)

    own_grads = jnp.concatenate(
        [dot(back_spread, acts, 0, 0), lowrank_scale * dot(low_spread, grads, 0, 0)], axis=1
    )
    own_grads = lax.psum(own_grads, "dp").astype(BF16)
    home = lax.all_to_all(
        own_grads.reshape(tensor_count, own_rows, ff_dev + d_dev),
        "tensor", split_axis=0, concat_axis=0, tiled=True,
    )
    down_own = home[:, :, :ff_dev].transpose(1, 0, 2).reshape(adapter_down.shape)
    up_own = home[:, :, ff_dev:].transpose(1, 0, 2).reshape(adapter_up.shape)

    layer = (base + lowrank_scale * dot(low_spread, up_all, 1, 0)).astype(BF16)
    layer_out = dot(place, layer, 0, 0).astype(BF16)
    return layer_out, grad_input, down_own, up_own


def solution(mesh):
    in_specs = (
        P(("groups", "dp"), "tensor"),
        P("tensor", None),
        P(("groups", "tensor"), None, None),
        P(("groups", "tensor"), None, None),
        P(("groups", "dp"), None),
        P(("groups", "dp"), None),
        P(("groups", "dp"), "tensor"),
    )
    out_specs = (
        P(("groups", "dp"), "tensor"),
        P(("groups", "dp"), "tensor"),
        P(("groups", "tensor"), None, None),
        P(("groups", "tensor"), None, None),
    )
    return jax.shard_map(body, mesh=mesh, in_specs=in_specs, out_specs=out_specs, check_vma=False)
```
